32 devices in a mesh: dp: 4 (over y, x), fsdp: 8 (over z, core).
Axes of the slice: x: 2, y: 2, z: 4, core: 2. Of those that a mesh axis runs over, the one named last changes fastest.
Arguments:
- images: bfloat16 [512, 197, 384], P(('dp', 'fsdp')), may hold values from -6 to 6
- counts: int32 [32], P(('dp', 'fsdp')), may hold values from 15 to 16
- qkv_flat: bfloat16 [442368], P(('dp', 'fsdp')), may hold values from -0.3125 to 0.3125
- out_flat: bfloat16 [147456], P(('dp', 'fsdp')), may hold values from -1.25 to 1.25
- up_flat: bfloat16 [589824], P(('dp', 'fsdp')), may hold values from -0.3125 to 0.3125
- down_flat: bfloat16 [589824], P(('dp', 'fsdp')), may hold values from -0.15625 to 0.15625
- vectors: bfloat16 [4608], P(('dp', 'fsdp')), may hold values from -1.5 to 1.5, as said below
- cotangent: bfloat16 [512, 197, 384], P(('dp', 'fsdp')), may hold values from -6 to 6
Outputs:
- block_out: bfloat16 [512, 197, 384], P(('dp', 'fsdp'))
- input_grad: float32 [512, 197, 384], P(('dp', 'fsdp'))
- grad_qkv: float32 [442368], P(('dp', 'fsdp'))
- grad_out: float32 [147456], P(('dp', 'fsdp'))
- grad_up: float32 [589824], P(('dp', 'fsdp'))
- grad_down: float32 [589824], P(('dp', 'fsdp'))
- grad_vectors: float32 [4608], P(('dp', 'fsdp'))
The draws below stay inside these ranges and needn't reach their ends.
Inputs may be any that keep to these rules, and one draw needn't show every extreme that they name: `counts`: slots at or past a device's count hold no image; their rows are ignored. `vectors`: the two norms' gains lie in 0.5 to 1.5.
All inputs are finite; a program needn't handle non-finite values.
Results may differ from the reference program's by a relative error of at most 0.009.
Values may be sent and summed in bfloat16 or wider, within the bound.
A program may use at most 192 MiB of HBM per device.

```python
import jax
import jax.numpy as jnp
from jax import lax

D = 384
HEADS = 6
HD = 64
FF = 1536
S = 197
IMG_DEV = 16
IMAGES = 512
DEVICES = 32


def draw_vectors(key, part):
    places = jnp.arange(8 * D + FF)
    key_gain, key_bias = jax.random.split(key)
    gain_draw = jax.random.uniform(key_gain, (8 * D + FF,), jnp.float32, 0.5, 1.5)
    biases = 0.3 * jax.random.truncated_normal(key_bias, -5.0, 5.0, (8 * D + FF,), jnp.float32)
    is_gain = (places < D) | (places >= 2 * D) & (places < 3 * D)
    return jnp.where(is_gain, gain_draw, biases).astype(jnp.bfloat16)


def set_ends(entries, rng, least, largest):
    extent = entries.shape
    place = [jax.random.randint(jax.random.fold_in(rng, axis), (), 0, extent[axis]) for axis in range(len(extent))]
    entries = entries.at[tuple(place)].set(least)
    longest = extent.index(max(extent))
    place[longest] = (place[longest] + 1) % extent[longest]
    return entries.at[tuple(place)].set(largest)


def block_scale(own_key, extent, shards, low, largest):
    loudness, own = 1.0, jax.random.fold_in(own_key, 6)
    for position, blocks in shards:
        heights = jnp.exp(jax.random.uniform(jax.random.fold_in(own, position), (blocks,), jnp.float32, low / len(shards), largest / len(shards)))
        loudness = loudness * jnp.repeat(heights, extent[position] // blocks).reshape([-1 if axis == position else 1 for axis in range(len(extent))])
    return loudness


def scatter_about(rng, shape, width, limit, cuts=(), kind=jnp.bfloat16):
    level = block_scale(rng, shape, cuts, -0.22, 0.18) if cuts else 1.0
    result = jax.random.normal(rng, shape, jnp.float32) * width * level
    return jnp.minimum(jnp.maximum(result, -limit), limit).astype(kind)


def setup_inputs(seed: int = 0) -> dict:
    splits = jax.random.split(jax.random.key(seed), 9)
    return {
        "images": scatter_about(splits[0], (IMAGES, S, D), 1.0, 6.0, ((0, 32),)),
        "counts": set_ends(jax.random.randint(splits[1], (DEVICES,), IMG_DEV - 1, IMG_DEV + 1), jax.random.fold_in(splits[1], 1), IMG_DEV - 1, IMG_DEV).astype(jnp.int32),
        "qkv_flat": scatter_about(splits[2], (3 * D * D,), D ** -0.5, 0.3125, ((0, 32),)),
        "out_flat": scatter_about(splits[3], (D * D,), (D // 16) ** -0.5, 1.25, ((0, 32),)),
        "up_flat": scatter_about(splits[4], (D * FF,), D ** -0.5, 0.3125, ((0, 32),)),
        "down_flat": scatter_about(splits[5], (FF * D,), FF ** -0.5, 0.15625, ((0, 32),)),
        "vectors": draw_vectors(jax.random.fold_in(splits[8], 71), 0),
        "cotangent": scatter_about(splits[7], (IMAGES, S, D), 1.0, 6.0, ((0, 32),)),
    }


epsilon = 1e-06

@jax.custom_vjp
def low(v):
    return lax.optimization_barrier(v.astype(jnp.bfloat16)).astype(jnp.float32)

@jax.custom_vjp
def low_back(v):
    return v

def low_keep(v):
    return (low(v), None)

def low_pass(kept, grad):
    return (grad,)

def back_keep(v):
    return (v, None)

def back_low(kept, grad):
    return (low(grad),)
low.defvjp(low_keep, low_pass)
low_back.defvjp(back_keep, back_low)

def layer_norm(rows, gain, shift):
    center = rows - lax.optimization_barrier(jnp.mean(rows, axis=-1, keepdims=True))
    return center * lax.rsqrt(lax.optimization_barrier(jnp.mean(center * center, axis=-1, keepdims=True)) + epsilon) * gain + shift

def product(left, right):
    return jnp.dot(left, right, precision=lax.Precision.HIGHEST)

def forward(rows, qkv_flat, out_flat, up_flat, down_flat, vectors, row_valid):
    slot_count = rows.shape[0] // S
    pieces = [vectors[block_index * D:(block_index + 1) * D] for block_index in range(8)]
    gain_one, shift_one, gain_two, shift_two, query_bias, value_bias, out_bias, down_bias = pieces
    up_bias = vectors[8 * D:]
    attention_input = low(layer_norm(rows, gain_one, shift_one))
    qkv_bias = jnp.concatenate([query_bias, jnp.zeros((D,), jnp.float32), value_bias])
    projected = low(low_back(product(attention_input, qkv_flat.reshape(D, 3 * D)) + qkv_bias))
    projected = projected.reshape(slot_count, S, 3, HEADS, HD)
    query_rows = projected[:, :, 0]
    key_rows = projected[:, :, 1]
    value_rows = projected[:, :, 2]
    scores = low_back(jnp.einsum('bqhd,bkhd->bhqk', query_rows, key_rows, precision=lax.Precision.HIGHEST) * HD ** (-0.5))
    row_max = lax.optimization_barrier(jnp.max(scores, axis=-1, keepdims=True))
    weights_exp = jnp.exp(scores - row_max)
    attention = weights_exp / lax.optimization_barrier(jnp.sum(weights_exp, axis=-1, keepdims=True))
    mixed = jnp.einsum('bhqk,bkhd->bqhd', low(attention), value_rows, precision=lax.Precision.HIGHEST)
    mixed_low = low(low_back(mixed)).reshape(-1, D)
    residual = rows + low_back(product(mixed_low, out_flat.reshape(D, D)) + out_bias)
    hidden_input = low(layer_norm(residual, gain_two, shift_two))
    up_sum = low_back(product(hidden_input, up_flat.reshape(D, FF)) + up_bias)
    activated = low(jax.nn.gelu(up_sum, approximate=False))
    block_sum = residual + low_back(product(activated, down_flat.reshape(FF, D)) + down_bias)
    return block_sum * row_valid

def reference(images, counts, qkv_flat, out_flat, up_flat, down_flat, vectors, cotangent):
    groups = IMAGES // IMG_DEV
    image_groups = images.astype(jnp.float32).reshape(groups, IMG_DEV * S, D)
    cotangent_groups = cotangent.astype(jnp.float32).reshape(groups, IMG_DEV * S, D)
    params = (qkv_flat.astype(jnp.float32), out_flat.astype(jnp.float32), up_flat.astype(jnp.float32), down_flat.astype(jnp.float32), vectors.astype(jnp.float32))

    def group_step(running, group_item):
        block_rows, block_cot, count_value = group_item
        slot_valid = (jnp.arange(IMG_DEV, dtype=jnp.int32) < count_value).astype(jnp.float32)
        row_valid = jnp.repeat(slot_valid, S)[:, None]

        def apply_block(rows, first_w, second_w, third_w, fourth_w, fifth_w):
            return forward(rows, first_w, second_w, third_w, fourth_w, fifth_w, row_valid)
        output, pullback = jax.vjp(apply_block, block_rows, params[0], params[1], params[2], params[3], params[4])
        gradients = pullback(block_cot)
        running = tuple((previous + update for previous, update in zip(running, gradients[1:])))
        return (running, (output, gradients[0]))
    zeros_init = tuple((jnp.zeros_like(param_value) for param_value in params))
    running, (outputs, input_grads) = lax.scan(group_step, zeros_init, (image_groups, cotangent_groups, counts))
    return (outputs.reshape(IMAGES, S, D).astype(jnp.bfloat16), input_grads.reshape(IMAGES, S, D), running[0], running[1], running[2], running[3], running[4])
```

```python
import functools

import jax
import jax.numpy as jnp
from jax import lax
from jax.experimental import pallas as pl
from jax.experimental.pallas import tpu as pltpu
from jax.sharding import PartitionSpec as P

D = 384
HEADS = 6
HD = 64
FF = 1536
EPS = 1e-06
AXES = ("dp", "fsdp")
GROUP = 2
CHUNK = 384
PAIR = 2 * HD
F32 = jnp.float32
BF16 = jnp.bfloat16


def dot(a, b, contract=((1,), (0,))):
    return lax.dot_general(a, b, (contract, ((), ())), preferred_element_type=F32)


def dot_t(a, b):
    return dot(a, b, ((1,), (1,)))


def normalize(rows):
    center = rows - jnp.mean(rows, axis=-1, keepdims=True)
    inverse = lax.rsqrt(jnp.mean(center * center, axis=-1, keepdims=True) + EPS)
    return center * inverse, inverse


def norm_back(upstream, normed, inverse, gain):
    scaled = upstream * gain
    first = jnp.mean(scaled, axis=-1, keepdims=True)
    second = jnp.mean(scaled * normed, axis=-1, keepdims=True)
    return inverse * (scaled - first - normed * second)


def column_sum(rows):
    return jnp.sum(rows, axis=0, keepdims=True)


def kernel(
    length, padded, counts, x_ref, ct_ref, wqkv, wout, wup, wdown, vec,
    block_out, input_grad, gqkv, gout, gup, gdown, gvec,
    aqkv, aout, aup, adown, avec, xs, es, qkv_s, mix_s, dmix_s, dqkv_s, p_s,
):
    step = pl.program_id(0)

    @pl.when(step == 0)
    def _():
        for ref in (aqkv, aout, aup, adown, avec, xs, es):
            ref[...] = jnp.zeros_like(ref)

    count = counts[0]
    for i in range(GROUP):
        valid = (step * GROUP + i < count).astype(F32)
        xs[i * padded : i * padded + length, :] = x_ref[i].astype(F32)
        es[i * padded : i * padded + length, :] = ct_ref[i].astype(F32) * valid

    def piece(k):
        return vec[:, k * D : (k + 1) * D]

    g1, c1, g2, c2, bq, bv, bo, bd = [piece(k) for k in range(8)]
    bias = jnp.concatenate([bq, jnp.zeros_like(bq), bv], axis=1)

    def add_vec(k, rows):
        avec[:, k * D : (k + 1) * D] += rows

    n1, inv1 = normalize(xs[...])
    a1 = (n1 * g1 + c1).astype(BF16)
    qkv_s[...] = (dot(a1, wqkv[...]) + bias).astype(BF16)

    first_half = lax.broadcasted_iota(jnp.int32, (padded, PAIR), 1) < HD
    key_ok = lax.broadcasted_iota(jnp.int32, (2 * padded, padded), 1) < length

    def stack(rows):
        zero = jnp.zeros_like(rows)
        return jnp.concatenate(
            [jnp.where(first_half, rows, zero), jnp.where(first_half, zero, rows)], axis=0
        )

    def unstack(rows):
        return jnp.where(first_half, rows[:padded], rows[padded:])

    def part(ref, i, which, pair):
        start = which * D + pair * PAIR
        return ref[i * padded : (i + 1) * padded, start : start + PAIR]

    scale = HD ** (-0.5)
    for i in range(GROUP):
        for pair in range(HEADS // 2):
            q = stack(part(qkv_s, i, 0, pair) * scale)
            scores = dot_t(q, part(qkv_s, i, 1, pair))
            scores = jnp.where(key_ok, scores, -1e30)
            e = jnp.exp(scores - jnp.max(scores, axis=-1, keepdims=True))
            p = e * (1.0 / jnp.sum(e, axis=-1, keepdims=True))
            p_s[i * (HEADS // 2) + pair] = p
            mixed = dot(p.astype(BF16), part(qkv_s, i, 2, pair))
            mix_s[i * padded : (i + 1) * padded, pair * PAIR : (pair + 1) * PAIR] = unstack(
                mixed
            ).astype(BF16)

    mix = mix_s[...]
    residual = xs[...] + dot(mix, wout[...]) + bo
    n2, inv2 = normalize(residual)
    a2 = (n2 * g2 + c2).astype(BF16)
    a2_t = a2.T
    e_low = es[...].astype(BF16)
    e_low_t = e_low.T
    total = residual + bd
    back = jnp.zeros_like(total)
    for c in range(FF // CHUNK):
        cols = slice(c * CHUNK, (c + 1) * CHUNK)
        vcols = slice(8 * D + c * CHUNK, 8 * D + (c + 1) * CHUNK)
        u = dot(a2, wup[:, cols]) + vec[:, vcols]
        cdf = 0.5 + 0.5 * lax.erf(u * (0.5**0.5))
        act = (u * cdf).astype(BF16)
        pdf = jnp.exp(-0.5 * u * u) * 0.3989422804014327
        du = dot_t(e_low, wdown[cols, :]) * (cdf + u * pdf)
        du_low = du.astype(BF16)
        total = total + dot(act, wdown[cols, :])
        back = back + dot_t(du_low, wup[:, cols])
        aup[:, cols] += dot(a2_t, du_low)
        adown[:, cols] += dot(e_low_t, act)
        avec[:, vcols] += column_sum(du_low.astype(F32))
    for i in range(GROUP):
        keep = step * GROUP + i < count
        rows = total[i * padded : i * padded + length]
        block_out[i] = jnp.where(keep, rows, 0.0).astype(BF16)
    add_vec(7, column_sum(e_low.astype(F32)))
    add_vec(2, column_sum(back * n2))
    add_vec(3, column_sum(back))
    dr = es[...] + norm_back(back, n2, inv2, g2)
    dr_low = dr.astype(BF16)
    es[...] = dr
    aout[...] += dot(mix.T, dr_low)
    add_vec(6, column_sum(dr_low.astype(F32)))
    dmix_s[...] = dot_t(dr_low, wout[...]).astype(BF16)

    for i in range(GROUP):
        rows = slice(i * padded, (i + 1) * padded)
        for pair in range(HEADS // 2):
            q = stack(part(qkv_s, i, 0, pair) * scale)
            k = part(qkv_s, i, 1, pair)
            do = stack(part(dmix_s, i, 0, pair))
            p = p_s[i * (HEADS // 2) + pair]
            dp = dot_t(do, part(qkv_s, i, 2, pair))
            ds = (p * (dp - jnp.sum(dp * p, axis=-1, keepdims=True))).astype(BF16)
            dv = dot(p.astype(BF16).T, do)
            dk = dot(ds.T, q)
            dq = unstack(dot(ds, k)) * scale
            for which, value in enumerate((dq, dk, dv)):
                start = which * D + pair * PAIR
                dqkv_s[rows, start : start + PAIR] = value.astype(BF16)

    dqkv = dqkv_s[...]
    aqkv[...] += dot(a1.T, dqkv)
    add_vec(4, column_sum(dqkv[:, :D].astype(F32)))
    add_vec(5, column_sum(dqkv[:, 2 * D :].astype(F32)))
    back1 = dot_t(dqkv, wqkv[...])
    add_vec(0, column_sum(back1 * n1))
    add_vec(1, column_sum(back1))
    dx = es[...] + norm_back(back1, n1, inv1, g1)
    for i in range(GROUP):
        input_grad[i] = dx[i * padded : i * padded + length]
    for i in range(GROUP):
        es[i * padded + length : (i + 1) * padded, :] = jnp.zeros((padded - length, D), F32)

    @pl.when(step == pl.num_programs(0) - 1)
    def _():
        gqkv[...] = aqkv[...].astype(BF16)
        gout[...] = aout[...].astype(BF16)
        gup[...] = aup[...].astype(BF16)
        gdown[...] = adown[...].T.astype(BF16)
        gvec[...] = avec[...]


def block(images, counts, weights, vec, cotangent):
    slots, length, _ = images.shape
    padded = -(-length // 16) * 16
    rows = GROUP * padded
    image_spec = pl.BlockSpec((GROUP, length, D), lambda s: (s, 0, 0))

    def whole(shape):
        return pl.BlockSpec(shape, lambda s: (0, 0))

    shapes = [(D, 3 * D), (D, D), (D, FF), (FF, D)]
    vec_shape = (1, 8 * D + FF)
    flops = 3 * 2 * slots * length * (3 * D * D + D * D + 2 * D * FF)
    return pl.pallas_call(
        functools.partial(kernel, length, padded),
        grid=(slots // GROUP,),
        in_specs=[pl.BlockSpec(memory_space=pltpu.SMEM), image_spec, image_spec]
        + [whole(s) for s in shapes]
        + [whole(vec_shape)],
        out_specs=[image_spec, image_spec] + [whole(s) for s in shapes] + [whole(vec_shape)],
        out_shape=[
            jax.ShapeDtypeStruct(images.shape, BF16),
            jax.ShapeDtypeStruct(images.shape, F32),
        ]
        + [jax.ShapeDtypeStruct(s, BF16) for s in shapes]
        + [jax.ShapeDtypeStruct(vec_shape, F32)],
        scratch_shapes=[
            pltpu.VMEM((D, 3 * D), F32),
            pltpu.VMEM((D, D), F32),
            pltpu.VMEM((D, FF), F32),
            pltpu.VMEM((D, FF), F32),
            pltpu.VMEM(vec_shape, F32),
            pltpu.VMEM((rows, D), F32),
            pltpu.VMEM((rows, D), F32),
            pltpu.VMEM((rows, 3 * D), BF16),
            pltpu.VMEM((rows, D), BF16),
            pltpu.VMEM((rows, D), BF16),
            pltpu.VMEM((rows, 3 * D), BF16),
            pltpu.VMEM((GROUP * HEADS // 2, 2 * padded, padded), F32),
        ],
        compiler_params=pltpu.CompilerParams(vmem_limit_bytes=56 * 2**20),
        cost_estimate=pl.CostEstimate(flops=flops, bytes_accessed=20 * 2**20, transcendentals=0),
    )(counts, images, cotangent, *weights, vec)


def stage_orders(dp, fsdp):
    inner = fsdp.bit_length() - 1
    outer = dp.bit_length() - 1
    z = list(range(1, inner))
    near = list(range(inner, inner + outer // 2))
    far = list(range(inner + outer // 2, inner + outer))
    return ([0] + near + far + z, [0] + far + z + near, [0] + z + near + far), inner + outer


def swap(value, bit, devices):
    return lax.ppermute(value, AXES, [(d, d ^ (1 << bit)) for d in range(devices)])


def gather(value, order, bits, me):
    held = value.reshape((1,) * bits + value.shape)
    for bit in reversed(order):
        other = swap(held, bit, 1 << bits)
        axis = bits - 1 - bit
        upper = (me >> bit) & 1
        held = jnp.where(
            upper == 1,
            jnp.concatenate([other, held], axis=axis),
            jnp.concatenate([held, other], axis=axis),
        )
    return held.reshape((1 << bits,) + value.shape)


def reduce_scatter(value, order, bits, me):
    held = value.reshape((2,) * bits + value.shape[1:])
    for bit in order:
        axis = bits - 1 - bit
        upper = (me >> bit) & 1
        sent = lax.dynamic_index_in_dim(held, 1 - upper, axis, keepdims=True)
        kept = lax.dynamic_index_in_dim(held, upper, axis, keepdims=True)
        got = swap(sent.astype(BF16), bit, 1 << bits)
        total = kept.astype(F32) + got.astype(F32)
        held = total if bit == order[-1] else total.astype(BF16)
    return held.reshape(value.shape[1:])


def make_body(dp, fsdp):
    devices = dp * fsdp
    orders, bits = stage_orders(dp, fsdp)
    rows_each = D // devices if D % devices == 0 else None

    def body(images, counts, qkv_flat, out_flat, up_flat, down_flat, vectors, cotangent):
        me = lax.axis_index(AXES)

        def shard(flat, width):
            return flat if rows_each is None else flat.reshape(rows_each, width)

        first = jnp.concatenate([shard(qkv_flat, 3 * D), shard(out_flat, D)], axis=-1)
        parts = [first, shard(up_flat, FF), shard(down_flat, FF)]
        first, up, down = [gather(v, o, bits, me) for v, o in zip(parts, orders)]
        vec = gather(vectors, orders[0], bits, me)
        cut = qkv_flat.shape[0] if rows_each is None else 3 * D
        weights = [
            first[..., :cut].reshape(D, 3 * D),
            first[..., cut:].reshape(D, D),
            up.reshape(D, FF),
            down.reshape(FF, D),
        ]
        vec = vec.astype(F32).reshape(1, -1)
        block_out, input_grad, gqkv, gout, gup, gdown, gvec = block(
            images, counts, weights, vec, cotangent
        )

        def blocks(grad, width):
            if rows_each is None:
                return grad.reshape(devices, -1)
            return grad.reshape(devices, rows_each, width)

        gfirst = jnp.concatenate([blocks(gqkv, 3 * D), blocks(gout, D)], axis=-1)
        grads = [gfirst, blocks(gup, FF), blocks(gdown, FF)]
        gfirst, gup, gdown = [reduce_scatter(g, o, bits, me) for g, o in zip(grads, orders)]
        gvec = reduce_scatter(gvec.reshape(devices, -1), orders[0], bits, me)
        return (
            block_out,
            input_grad,
            gfirst[..., :cut].reshape(-1),
            gfirst[..., cut:].reshape(-1),
            gup.reshape(-1),
            gdown.reshape(-1),
            gvec,
        )

    return body


def solution(mesh):
    split = P(AXES)
    image = P(AXES, None, None)
    return jax.shard_map(
        make_body(mesh.shape["dp"], mesh.shape["fsdp"]),
        mesh=mesh,
        in_specs=(image, split, split, split, split, split, split, image),
        out_specs=(image, image, split, split, split, split, split),
        check_vma=False,
    )
```

```python
import functools

import jax
import jax.numpy as jnp
from jax import lax
from jax.experimental import pallas as pl
from jax.experimental.pallas import tpu as pltpu
from jax.sharding import PartitionSpec as P

D = 384
HEADS = 6
HD = 64
FF = 1536
EPS = 1e-06
AXES = ("dp", "fsdp")
GROUP = 2
CHUNK = 384
PAIR = 2 * HD
BLOCKS = 32
ROWS = D // BLOCKS
F32 = jnp.float32
BF16 = jnp.bfloat16


def dot(a, b, contract=((1,), (0,))):
    return lax.dot_general(a, b, (contract, ((), ())), preferred_element_type=F32)


def dot_t(a, b):
    return dot(a, b, ((1,), (1,)))


def normalize(rows):
    center = rows - jnp.mean(rows, axis=-1, keepdims=True)
    inverse = lax.rsqrt(jnp.mean(center * center, axis=-1, keepdims=True) + EPS)
    return center * inverse, inverse


def norm_back(upstream, normed, inverse, gain):
    scaled = upstream * gain
    first = jnp.mean(scaled, axis=-1, keepdims=True)
    second = jnp.mean(scaled * normed, axis=-1, keepdims=True)
    return inverse * (scaled - first - normed * second)


def column_sum(rows):
    return jnp.sum(rows, axis=0, keepdims=True)


def kernel(
    length, padded, counts, x_ref, ct_ref, wfirst, wup_in, wdown, vec,
    block_out, input_grad, gfirst, gup, gdown, gvec,
    wqkv, wout, wup, aqkv, aout, aup, adown, avec, xs, es, qkv_s, mix_s, dmix_s, dqkv_s, p_s,
):
    step = pl.program_id(0)

    @pl.when(step == 0)
    def _():
        for ref in (aqkv, aout, aup, adown, avec, xs, es):
            ref[...] = jnp.zeros_like(ref)
        for at in range(0, BLOCKS, 4):
            rows = slice(at * ROWS, (at + 4) * ROWS)
            for ref, outs in ((wfirst, (wqkv, wout)), (wup_in, (wup,))):
                joined = jnp.concatenate([ref[at + k].astype(F32) for k in range(4)], axis=0)
                joined = joined.astype(BF16)
                if len(outs) == 1:
                    wup[rows, :] = joined
                else:
                    wqkv[rows, :] = joined[:, : 3 * D]
                    wout[rows, :] = joined[:, 3 * D :]

    count = counts[0]
    for i in range(GROUP):
        valid = (step * GROUP + i < count).astype(F32)
        xs[i * padded : i * padded + length, :] = x_ref[i].astype(F32)
        es[i * padded : i * padded + length, :] = ct_ref[i].astype(F32) * valid

    def piece(k):
        return vec[:, k * D : (k + 1) * D]

    g1, c1, g2, c2, bq, bv, bo, bd = [piece(k) for k in range(8)]
    bias = jnp.concatenate([bq, jnp.zeros_like(bq), bv], axis=1)

    def add_vec(k, rows):
        avec[:, k * D : (k + 1) * D] += rows

    n1, inv1 = normalize(xs[...])
    a1 = (n1 * g1 + c1).astype(BF16)
    qkv_s[...] = (dot(a1, wqkv[...]) + bias).astype(BF16)

    first_half = lax.broadcasted_iota(jnp.int32, (padded, PAIR), 1) < HD
    key_ok = lax.broadcasted_iota(jnp.int32, (2 * padded, padded), 1) < length

    def stack(rows):
        zero = jnp.zeros_like(rows)
        return jnp.concatenate(
            [jnp.where(first_half, rows, zero), jnp.where(first_half, zero, rows)], axis=0
        )

    def unstack(rows):
        return jnp.where(first_half, rows[:padded], rows[padded:])

    def part(ref, i, which, pair):
        start = which * D + pair * PAIR
        return ref[i * padded : (i + 1) * padded, start : start + PAIR]

    scale = HD ** (-0.5)
    for i in range(GROUP):
        for pair in range(HEADS // 2):
            q = stack(part(qkv_s, i, 0, pair) * scale)
            scores = dot_t(q, part(qkv_s, i, 1, pair))
            scores = jnp.where(key_ok, scores, -1e30)
            e = jnp.exp(scores - jnp.max(scores, axis=-1, keepdims=True))
            p = e * (1.0 / jnp.sum(e, axis=-1, keepdims=True))
            p_s[i * (HEADS // 2) + pair] = p
            mixed = dot(p.astype(BF16), part(qkv_s, i, 2, pair))
            mix_s[i * padded : (i + 1) * padded, pair * PAIR : (pair + 1) * PAIR] = unstack(
                mixed
            ).astype(BF16)

    mix = mix_s[...]
    residual = xs[...] + dot(mix, wout[...]) + bo
    n2, inv2 = normalize(residual)
    a2 = (n2 * g2 + c2).astype(BF16)
    a2_t = a2.T
    e_low = es[...].astype(BF16)
    e_low_t = e_low.T
    total = residual + bd
    back = jnp.zeros_like(total)
    for c in range(FF // CHUNK):
        cols = slice(c * CHUNK, (c + 1) * CHUNK)
        vcols = slice(8 * D + c * CHUNK, 8 * D + (c + 1) * CHUNK)
        u = dot(a2, wup[:, cols]) + vec[:, vcols]
        cdf = 0.5 + 0.5 * lax.erf(u * (0.5**0.5))
        act = (u * cdf).astype(BF16)
        pdf = jnp.exp(-0.5 * u * u) * 0.3989422804014327
        du = dot_t(e_low, wdown[cols, :]) * (cdf + u * pdf)
        du_low = du.astype(BF16)
        total = total + dot(act, wdown[cols, :])
        back = back + dot_t(du_low, wup[:, cols])
        aup[:, cols] += dot(a2_t, du_low)
        adown[:, cols] += dot(e_low_t, act)
        avec[:, vcols] += column_sum(du_low.astype(F32))
    for i in range(GROUP):
        keep = step * GROUP + i < count
        rows = total[i * padded : i * padded + length]
        block_out[i] = jnp.where(keep, rows, 0.0).astype(BF16)
    add_vec(7, column_sum(e_low.astype(F32)))
    add_vec(2, column_sum(back * n2))
    add_vec(3, column_sum(back))
    dr = es[...] + norm_back(back, n2, inv2, g2)
    dr_low = dr.astype(BF16)
    es[...] = dr
    aout[...] += dot(mix.T, dr_low)
    add_vec(6, column_sum(dr_low.astype(F32)))
    dmix_s[...] = dot_t(dr_low, wout[...]).astype(BF16)

    for i in range(GROUP):
        rows = slice(i * padded, (i + 1) * padded)
        for pair in range(HEADS // 2):
            q = stack(part(qkv_s, i, 0, pair) * scale)
            k = part(qkv_s, i, 1, pair)
            do = stack(part(dmix_s, i, 0, pair))
            p = p_s[i * (HEADS // 2) + pair]
            dp = dot_t(do, part(qkv_s, i, 2, pair))
            ds = (p * (dp - jnp.sum(dp * p, axis=-1, keepdims=True))).astype(BF16)
            dv = dot(p.astype(BF16).T, do)
            dk = dot(ds.T, q)
            dq = unstack(dot(ds, k)) * scale
            for which, value in enumerate((dq, dk, dv)):
                start = which * D + pair * PAIR
                dqkv_s[rows, start : start + PAIR] = value.astype(BF16)

    dqkv = dqkv_s[...]
    aqkv[...] += dot(a1.T, dqkv)
    add_vec(4, column_sum(dqkv[:, :D].astype(F32)))
    add_vec(5, column_sum(dqkv[:, 2 * D :].astype(F32)))
    back1 = dot_t(dqkv, wqkv[...])
    add_vec(0, column_sum(back1 * n1))
    add_vec(1, column_sum(back1))
    dx = es[...] + norm_back(back1, n1, inv1, g1)
    for i in range(GROUP):
        input_grad[i] = dx[i * padded : i * padded + length]
    for i in range(GROUP):
        es[i * padded + length : (i + 1) * padded, :] = jnp.zeros((padded - length, D), F32)

    @pl.when(step == pl.num_programs(0) - 1)
    def _():
        for at in range(0, BLOCKS, 4):
            rows = slice(at * ROWS, (at + 4) * ROWS)
            first = jnp.concatenate([aqkv[rows, :], aout[rows, :]], axis=1)
            up = aup[rows, :]
            for k in range(4):
                own = slice(k * ROWS, (k + 1) * ROWS)
                gfirst[at + k] = first[own].astype(BF16)
                gup[at + k] = up[own].astype(BF16)
        gdown[...] = adown[...].T.astype(BF16)
        gvec[...] = avec[...]


def block(images, counts, weights, vec, cotangent):
    slots, length, _ = images.shape
    padded = -(-length // 16) * 16
    rows = GROUP * padded
    image_spec = pl.BlockSpec((GROUP, length, D), lambda s: (s, 0, 0))

    def whole(shape):
        return pl.BlockSpec(shape, lambda s: (0,) * len(shape))

    shapes = [(BLOCKS, ROWS, 4 * D), (BLOCKS, ROWS, FF), (FF, D)]
    vec_shape = (1, 8 * D + FF)
    flops = 3 * 2 * slots * length * (3 * D * D + D * D + 2 * D * FF)
    return pl.pallas_call(
        functools.partial(kernel, length, padded),
        grid=(slots // GROUP,),
        in_specs=[pl.BlockSpec(memory_space=pltpu.SMEM), image_spec, image_spec]
        + [whole(s) for s in shapes]
        + [whole(vec_shape)],
        out_specs=[image_spec, image_spec] + [whole(s) for s in shapes] + [whole(vec_shape)],
        out_shape=[
            jax.ShapeDtypeStruct(images.shape, BF16),
            jax.ShapeDtypeStruct(images.shape, F32),
        ]
        + [jax.ShapeDtypeStruct(s, BF16) for s in shapes]
        + [jax.ShapeDtypeStruct(vec_shape, F32)],
        scratch_shapes=[
            pltpu.VMEM((D, 3 * D), BF16),
            pltpu.VMEM((D, D), BF16),
            pltpu.VMEM((D, FF), BF16),
            pltpu.VMEM((D, 3 * D), F32),
            pltpu.VMEM((D, D), F32),
            pltpu.VMEM((D, FF), F32),
            pltpu.VMEM((D, FF), F32),
            pltpu.VMEM(vec_shape, F32),
            pltpu.VMEM((rows, D), F32),
            pltpu.VMEM((rows, D), F32),
            pltpu.VMEM((rows, 3 * D), BF16),
            pltpu.VMEM((rows, D), BF16),
            pltpu.VMEM((rows, D), BF16),
            pltpu.VMEM((rows, 3 * D), BF16),
            pltpu.VMEM((GROUP * HEADS // 2, 2 * padded, padded), F32),
        ],
        compiler_params=pltpu.CompilerParams(vmem_limit_bytes=56 * 2**20),
        cost_estimate=pl.CostEstimate(flops=flops, bytes_accessed=20 * 2**20, transcendentals=0),
    )(counts, images, cotangent, *weights, vec)


def stage_orders(dp, fsdp):
    inner = fsdp.bit_length() - 1
    outer = dp.bit_length() - 1
    z = list(range(1, inner))
    near = list(range(inner, inner + outer // 2))
    far = list(range(inner + outer // 2, inner + outer))
    return ([0] + near + far + z, [0] + far + z + near, [0] + z + near + far), inner + outer


def swap(value, bit, devices):
    return lax.ppermute(value, AXES, [(d, d ^ (1 << bit)) for d in range(devices)])


def gather(value, order, bits, me):
    held = value.reshape((1,) * bits + value.shape)
    for bit in reversed(order):
        other = swap(held, bit, 1 << bits)
        axis = bits - 1 - bit
        upper = (me >> bit) & 1
        held = jnp.where(
            upper == 1,
            jnp.concatenate([other, held], axis=axis),
            jnp.concatenate([held, other], axis=axis),
        )
    return held.reshape((1 << bits,) + value.shape)


def reduce_scatter(value, order, bits, me):
    held = value.reshape((2,) * bits + value.shape[1:])
    for bit in order:
        axis = bits - 1 - bit
        upper = (me >> bit) & 1
        sent = lax.dynamic_index_in_dim(held, 1 - upper, axis, keepdims=True)
        kept = lax.dynamic_index_in_dim(held, upper, axis, keepdims=True)
        got = swap(sent.astype(BF16), bit, 1 << bits)
        total = kept.astype(F32) + got.astype(F32)
        held = total if bit == order[-1] else total.astype(BF16)
    return held.reshape(value.shape[1:])


def make_body(dp, fsdp):
    devices = dp * fsdp
    orders, bits = stage_orders(dp, fsdp)
    rows_each = D // devices if D % devices == 0 else None

    def body(images, counts, qkv_flat, out_flat, up_flat, down_flat, vectors, cotangent):
        me = lax.axis_index(AXES)

        def shard(flat, width):
            return flat if rows_each is None else flat.reshape(-1, width)

        first = jnp.concatenate([shard(qkv_flat, 3 * D), shard(out_flat, D)], axis=-1)
        parts = [first, shard(up_flat, FF), shard(down_flat, D)]
        first, up, down = [gather(v, o, bits, me) for v, o in zip(parts, orders)]
        vec = gather(vectors, orders[0], bits, me)
        cut = qkv_flat.shape[0] if rows_each is None else 3 * D
        if rows_each is None:
            pair = [first[:, :cut].reshape(D, 3 * D), first[:, cut:].reshape(D, D)]
            first = jnp.concatenate(pair, axis=1)
        weights = [
            first.reshape(BLOCKS, ROWS, 4 * D),
            up.reshape(BLOCKS, ROWS, FF),
            down.reshape(FF, D),
        ]
        vec = vec.astype(F32).reshape(1, -1)
        block_out, input_grad, gfirst, gup, gdown, gvec = block(
            images, counts, weights, vec, cotangent
        )
        if rows_each is None:
            both = gfirst.reshape(D, 4 * D)
            pair = [both[:, : 3 * D], both[:, 3 * D :]]
            gfirst = jnp.concatenate([g.reshape(devices, -1) for g in pair], axis=1)
            gup, gdown = [g.reshape(devices, -1) for g in (gup, gdown)]
        else:
            gfirst, gup = [g.reshape(devices, rows_each, 4 * D) for g in (gfirst, gup)]
            gdown = gdown.reshape(devices, -1, D)
        grads = [gfirst, gup, gdown]
        gfirst, gup, gdown = [reduce_scatter(g, o, bits, me) for g, o in zip(grads, orders)]
        gvec = reduce_scatter(gvec.reshape(devices, -1), orders[0], bits, me)
        return (
            block_out,
            input_grad,
            gfirst[..., :cut].reshape(-1),
            gfirst[..., cut:].reshape(-1),
            gup.reshape(-1),
            gdown.reshape(-1),
            gvec,
        )

    return body


def solution(mesh):
    split = P(AXES)
    image = P(AXES, None, None)
    return jax.shard_map(
        make_body(mesh.shape["dp"], mesh.shape["fsdp"]),
        mesh=mesh,
        in_specs=(image, split, split, split, split, split, split, image),
        out_specs=(image, image, split, split, split, split, split),
        check_vma=False,
    )
```

```python
import functools

import jax
import jax.numpy as jnp
from jax import lax
from jax.experimental import pallas as pl
from jax.experimental.pallas import tpu as pltpu
from jax.sharding import PartitionSpec as P

D = 384
HEADS = 6
HD = 64
FF = 1536
EPS = 1e-06
AXES = ("dp", "fsdp")
GROUP = 4
CHUNK = 384
PAIR = 2 * HD
BLOCKS = 32
ROWS = D // BLOCKS
F32 = jnp.float32
BF16 = jnp.bfloat16


def dot(a, b, contract=((1,), (0,))):
    return lax.dot_general(a, b, (contract, ((), ())), preferred_element_type=F32)


def dot_t(a, b):
    return dot(a, b, ((1,), (1,)))


def normalize(rows):
    center = rows - jnp.mean(rows, axis=-1, keepdims=True)
    inverse = lax.rsqrt(jnp.mean(center * center, axis=-1, keepdims=True) + EPS)
    return center * inverse, inverse


def norm_back(upstream, normed, inverse, gain):
    scaled = upstream * gain
    first = jnp.mean(scaled, axis=-1, keepdims=True)
    second = jnp.mean(scaled * normed, axis=-1, keepdims=True)
    return inverse * (scaled - first - normed * second)


def column_sum(rows):
    return jnp.sum(rows, axis=0, keepdims=True)


def kernel(
    length, padded, counts, x_ref, ct_ref, wfirst, wup_in, wdown, vec,
    block_out, input_grad, gfirst, gup, gdown, gvec,
    wqkv, wout, wup, aqkv, aout, aup, adown, avec, xs, es, qkv_s, mix_s, dmix_s, dqkv_s, p_s,
):
    step = pl.program_id(0)

    @pl.when(step == 0)
    def _():
        for ref in (aqkv, aout, aup, adown, avec, xs, es):
            ref[...] = jnp.zeros_like(ref)
        for at in range(0, BLOCKS, 4):
            rows = slice(at * ROWS, (at + 4) * ROWS)
            for ref, outs in ((wfirst, (wqkv, wout)), (wup_in, (wup,))):
                joined = jnp.concatenate([ref[at + k].astype(F32) for k in range(4)], axis=0)
                joined = joined.astype(BF16)
                if len(outs) == 1:
                    wup[rows, :] = joined
                else:
                    wqkv[rows, :] = joined[:, : 3 * D]
                    wout[rows, :] = joined[:, 3 * D :]

    count = counts[0]
    for i in range(GROUP):
        valid = (step * GROUP + i < count).astype(F32)
        xs[i * padded : i * padded + length, :] = x_ref[i].astype(F32)
        es[i * padded : i * padded + length, :] = ct_ref[i].astype(F32) * valid

    def piece(k):
        return vec[:, k * D : (k + 1) * D]

    g1, c1, g2, c2, bq, bv, bo, bd = [piece(k) for k in range(8)]
    bias = jnp.concatenate([bq, jnp.zeros_like(bq), bv], axis=1)

    def add_vec(k, rows):
        avec[:, k * D : (k + 1) * D] += rows

    n1, inv1 = normalize(xs[...])
    a1 = (n1 * g1 + c1).astype(BF16)
    qkv_s[...] = (dot(a1, wqkv[...]) + bias).astype(BF16)

    first_half = lax.broadcasted_iota(jnp.int32, (padded, PAIR), 1) < HD
    key_ok = lax.broadcasted_iota(jnp.int32, (2 * padded, padded), 1) < length

    def stack(rows):
        zero = jnp.zeros_like(rows)
        return jnp.concatenate(
            [jnp.where(first_half, rows, zero), jnp.where(first_half, zero, rows)], axis=0
        )

    def unstack(rows):
        return jnp.where(first_half, rows[:padded], rows[padded:])

    def part(ref, i, which, pair):
        start = which * D + pair * PAIR
        return ref[i * padded : (i + 1) * padded, start : start + PAIR]

    scale = HD ** (-0.5)
    for i in range(GROUP):
        for pair in range(HEADS // 2):
            q = stack(part(qkv_s, i, 0, pair) * scale)
            scores = dot_t(q, part(qkv_s, i, 1, pair))
            scores = jnp.where(key_ok, scores, -1e30)
            e = jnp.exp(scores - jnp.max(scores, axis=-1, keepdims=True))
            p = e * (1.0 / jnp.sum(e, axis=-1, keepdims=True))
            p_s[i * (HEADS // 2) + pair] = p
            mixed = dot(p.astype(BF16), part(qkv_s, i, 2, pair))
            mix_s[i * padded : (i + 1) * padded, pair * PAIR : (pair + 1) * PAIR] = unstack(
                mixed
            ).astype(BF16)

    mix = mix_s[...]
    residual = xs[...] + dot(mix, wout[...]) + bo
    n2, inv2 = normalize(residual)
    a2 = (n2 * g2 + c2).astype(BF16)
    a2_t = a2.T
    e_low = es[...].astype(BF16)
    e_low_t = e_low.T
    total = residual + bd
    back = jnp.zeros_like(total)
    for c in range(FF // CHUNK):
        cols = slice(c * CHUNK, (c + 1) * CHUNK)
        vcols = slice(8 * D + c * CHUNK, 8 * D + (c + 1) * CHUNK)
        u = dot(a2, wup[:, cols]) + vec[:, vcols]
        cdf = 0.5 + 0.5 * lax.erf(u * (0.5**0.5))
        act = (u * cdf).astype(BF16)
        pdf = jnp.exp(-0.5 * u * u) * 0.3989422804014327
        du = dot_t(e_low, wdown[cols, :]) * (cdf + u * pdf)
        du_low = du.astype(BF16)
        total = total + dot(act, wdown[cols, :])
        back = back + dot_t(du_low, wup[:, cols])
        aup[:, cols] += dot(a2_t, du_low)
        adown[:, cols] += dot(e_low_t, act)
        avec[:, vcols] += column_sum(du_low.astype(F32))
    for i in range(GROUP):
        keep = step * GROUP + i < count
        rows = total[i * padded : i * padded + length]
        block_out[i] = jnp.where(keep, rows, 0.0).astype(BF16)
    add_vec(7, column_sum(e_low.astype(F32)))
    add_vec(2, column_sum(back * n2))
    add_vec(3, column_sum(back))
    dr = es[...] + norm_back(back, n2, inv2, g2)
    dr_low = dr.astype(BF16)
    es[...] = dr
    aout[...] += dot(mix.T, dr_low)
    add_vec(6, column_sum(dr_low.astype(F32)))
    dmix_s[...] = dot_t(dr_low, wout[...]).astype(BF16)

    for i in range(GROUP):
        rows = slice(i * padded, (i + 1) * padded)
        for pair in range(HEADS // 2):
            q = stack(part(qkv_s, i, 0, pair) * scale)
            k = part(qkv_s, i, 1, pair)
            do = stack(part(dmix_s, i, 0, pair))
            p = p_s[i * (HEADS // 2) + pair]
            dp = dot_t(do, part(qkv_s, i, 2, pair))
            ds = (p * (dp - jnp.sum(dp * p, axis=-1, keepdims=True))).astype(BF16)
            dv = dot(p.astype(BF16).T, do)
            dk = dot(ds.T, q)
            dq = unstack(dot(ds, k)) * scale
            for which, value in enumerate((dq, dk, dv)):
                start = which * D + pair * PAIR
                dqkv_s[rows, start : start + PAIR] = value.astype(BF16)

    dqkv = dqkv_s[...]
    aqkv[...] += dot(a1.T, dqkv)
    add_vec(4, column_sum(dqkv[:, :D].astype(F32)))
    add_vec(5, column_sum(dqkv[:, 2 * D :].astype(F32)))
    back1 = dot_t(dqkv, wqkv[...])
    add_vec(0, column_sum(back1 * n1))
    add_vec(1, column_sum(back1))
    dx = es[...] + norm_back(back1, n1, inv1, g1)
    for i in range(GROUP):
        input_grad[i] = dx[i * padded : i * padded + length]
    for i in range(GROUP):
        es[i * padded + length : (i + 1) * padded, :] = jnp.zeros((padded - length, D), F32)

    @pl.when(step == pl.num_programs(0) - 1)
    def _():
        for at in range(0, BLOCKS, 4):
            rows = slice(at * ROWS, (at + 4) * ROWS)
            first = jnp.concatenate([aqkv[rows, :], aout[rows, :]], axis=1)
            up = aup[rows, :]
            for k in range(4):
                own = slice(k * ROWS, (k + 1) * ROWS)
                gfirst[at + k] = first[own].astype(BF16)
                gup[at + k] = up[own].astype(BF16)
        gdown[...] = adown[...].T.astype(BF16)
        gvec[...] = avec[...]


def block(images, counts, weights, vec, cotangent):
    slots, length, _ = images.shape
    padded = -(-length // 16) * 16
    rows = GROUP * padded
    image_spec = pl.BlockSpec((GROUP, length, D), lambda s: (s, 0, 0))

    def whole(shape):
        return pl.BlockSpec(shape, lambda s: (0,) * len(shape))

    shapes = [(BLOCKS, ROWS, 4 * D), (BLOCKS, ROWS, FF), (FF, D)]
    vec_shape = (1, 8 * D + FF)
    flops = 3 * 2 * slots * length * (3 * D * D + D * D + 2 * D * FF)
    return pl.pallas_call(
        functools.partial(kernel, length, padded),
        grid=(slots // GROUP,),
        in_specs=[pl.BlockSpec(memory_space=pltpu.SMEM), image_spec, image_spec]
        + [whole(s) for s in shapes]
        + [whole(vec_shape)],
        out_specs=[image_spec, image_spec] + [whole(s) for s in shapes] + [whole(vec_shape)],
        out_shape=[
            jax.ShapeDtypeStruct(images.shape, BF16),
            jax.ShapeDtypeStruct(images.shape, F32),
        ]
        + [jax.ShapeDtypeStruct(s, BF16) for s in shapes]
        + [jax.ShapeDtypeStruct(vec_shape, F32)],
        scratch_shapes=[
            pltpu.VMEM((D, 3 * D), BF16),
            pltpu.VMEM((D, D), BF16),
            pltpu.VMEM((D, FF), BF16),
            pltpu.VMEM((D, 3 * D), F32),
            pltpu.VMEM((D, D), F32),
            pltpu.VMEM((D, FF), F32),
            pltpu.VMEM((D, FF), F32),
            pltpu.VMEM(vec_shape, F32),
            pltpu.VMEM((rows, D), F32),
            pltpu.VMEM((rows, D), F32),
            pltpu.VMEM((rows, 3 * D), BF16),
            pltpu.VMEM((rows, D), BF16),
            pltpu.VMEM((rows, D), BF16),
            pltpu.VMEM((rows, 3 * D), BF16),
            pltpu.VMEM((GROUP * HEADS // 2, 2 * padded, padded), F32),
        ],
        compiler_params=pltpu.CompilerParams(vmem_limit_bytes=56 * 2**20),
        cost_estimate=pl.CostEstimate(flops=flops, bytes_accessed=20 * 2**20, transcendentals=0),
    )(counts, images, cotangent, *weights, vec)


def stage_orders(dp, fsdp):
    inner = fsdp.bit_length() - 1
    outer = dp.bit_length() - 1
    z = list(range(1, inner))
    near = list(range(inner, inner + outer // 2))
    far = list(range(inner + outer // 2, inner + outer))
    return ([0] + near + far + z, [0] + far + z + near, [0] + z + near + far), inner + outer


def swap(value, bit, devices):
    return lax.ppermute(value, AXES, [(d, d ^ (1 << bit)) for d in range(devices)])


def gather(value, order, bits, me):
    held = value.reshape((1,) * bits + value.shape)
    for bit in reversed(order):
        other = swap(held, bit, 1 << bits)
        axis = bits - 1 - bit
        upper = (me >> bit) & 1
        held = jnp.where(
            upper == 1,
            jnp.concatenate([other, held], axis=axis),
            jnp.concatenate([held, other], axis=axis),
        )
    return held.reshape((1 << bits,) + value.shape)


def reduce_scatter(value, order, bits, me):
    held = value.reshape((2,) * bits + value.shape[1:])
    for bit in order:
        axis = bits - 1 - bit
        upper = (me >> bit) & 1
        sent = lax.dynamic_index_in_dim(held, 1 - upper, axis, keepdims=True)
        kept = lax.dynamic_index_in_dim(held, upper, axis, keepdims=True)
        got = swap(sent.astype(BF16), bit, 1 << bits)
        total = kept.astype(F32) + got.astype(F32)
        held = total if bit == order[-1] else total.astype(BF16)
    return held.reshape(value.shape[1:])


def make_body(dp, fsdp):
    devices = dp * fsdp
    orders, bits = stage_orders(dp, fsdp)
    rows_each = D // devices if D % devices == 0 else None

    def body(images, counts, qkv_flat, out_flat, up_flat, down_flat, vectors, cotangent):
        me = lax.axis_index(AXES)

        def shard(flat, width):
            return flat if rows_each is None else flat.reshape(-1, width)

        first = jnp.concatenate([shard(qkv_flat, 3 * D), shard(out_flat, D)], axis=-1)
        parts = [first, shard(up_flat, FF), shard(down_flat, D)]
        first, up, down = [gather(v, o, bits, me) for v, o in zip(parts, orders)]
        vec = gather(vectors, orders[0], bits, me)
        cut = qkv_flat.shape[0] if rows_each is None else 3 * D
        if rows_each is None:
            pair = [first[:, :cut].reshape(D, 3 * D), first[:, cut:].reshape(D, D)]
            first = jnp.concatenate(pair, axis=1)
        weights = [
            first.reshape(BLOCKS, ROWS, 4 * D),
            up.reshape(BLOCKS, ROWS, FF),
            down.reshape(FF, D),
        ]
        vec = vec.astype(F32).reshape(1, -1)
        block_out, input_grad, gfirst, gup, gdown, gvec = block(
            images, counts, weights, vec, cotangent
        )
        if rows_each is None:
            both = gfirst.reshape(D, 4 * D)
            pair = [both[:, : 3 * D], both[:, 3 * D :]]
            gfirst = jnp.concatenate([g.reshape(devices, -1) for g in pair], axis=1)
            gup, gdown = [g.reshape(devices, -1) for g in (gup, gdown)]
        else:
            gfirst, gup = [g.reshape(devices, rows_each, 4 * D) for g in (gfirst, gup)]
            gdown = gdown.reshape(devices, -1, D)
        grads = [gfirst, gup, gdown]
        gfirst, gup, gdown = [reduce_scatter(g, o, bits, me) for g, o in zip(grads, orders)]
        gvec = reduce_scatter(gvec.reshape(devices, -1), orders[0], bits, me)
        return (
            block_out,
            input_grad,
            gfirst[..., :cut].reshape(-1),
            gfirst[..., cut:].reshape(-1),
            gup.reshape(-1),
            gdown.reshape(-1),
            gvec,
        )

    return body


def solution(mesh):
    split = P(AXES)
    image = P(AXES, None, None)
    return jax.shard_map(
        make_body(mesh.shape["dp"], mesh.shape["fsdp"]),
        mesh=mesh,
        in_specs=(image, split, split, split, split, split, split, image),
        out_specs=(image, image, split, split, split, split, split),
        check_vma=False,
    )
```
